32 devices in a mesh: groups: 2 (over x), col: 16 (over z, y, core).
Axes of the slice: x: 2, y: 2, z: 4, core: 2. Of those that a mesh axis runs over, the one named last changes fastest.
Arguments:
- blocks: bfloat16 [768, 128, 128], P('col'), may hold values from -0.15625 to 0.15625
- block_rows: int32 [768], P('col'), may hold values from 0 to 63, as said below
- block_cols: int32 [768], P('col'), may hold values from 0 to 127, as said below
- primal: float32 [16384, 256], P('col', 'groups'), parts along dimension 1, may hold values from -4 to 4
- dual: float32 [8192, 256], P('col', 'groups'), parts along dimension 1, may hold values from -4 to 4
- anchor_primal: float32 [16384, 256], P('col', 'groups'), parts along dimension 1, may hold values from -4 to 4
- anchor_dual: float32 [8192, 256], P('col', 'groups'), parts along dimension 1, may hold values from -4 to 4
- cost: float32 [16384, 256], P('col', 'groups'), parts along dimension 1, may hold values from -6 to 6
- rhs: float32 [8192, 256], P('col', 'groups'), parts along dimension 1, may hold values from -6 to 6
- bound_kind: int32 [16384, 256], P('col', 'groups'), parts along dimension 1, may hold values from 0 to 2
- lower: float32 [16384], P('col'), may hold values from -1.5 to -0.2
- upper: float32 [16384], P('col'), may hold values from 0.2 to 1.5
- step_size: float32 [256], P('groups'), parts along dimension 0, may hold values from 0.1 to 0.4
- primal_weight: float32 [256], P('groups'), parts along dimension 0, may hold values from 0.5 to 2
Outputs:
- primal_out: float32 [16384, 256], P('col', 'groups'), parts along dimension 1
- dual_out: float32 [8192, 256], P('col', 'groups'), parts along dimension 1
- fixed_point_residuals: float32 [3, 256], P(None, 'groups'), parts along dimension 1
The draws below stay inside these ranges and needn't reach their ends.
There are 2 independent parts, one for each index of `groups`. The reference program is written for one: setup_inputs(seed, part) draws one part's arguments, and reference() takes and returns one part's arrays. A program takes and returns all parts, laid end to end along the dimension named above; an argument that names none is the same for every part. Nothing has to cross between parts.
Inputs may be any that keep to these rules, and one draw needn't show every extreme that they name: `block_rows`: the blocks 48 * d to 48 * d + 47 lie in column blocks 8 * d to 8 * d + 7, and their row blocks are among the 4 row blocks of each of d - 1, d and d + 1 (counted cyclically, row block r belonging to r // 4); no pair of row and column block appears twice. `block_cols`: see block_rows; the column blocks of entries 48 * d to 48 * d + 47 are those of d.
All inputs are finite; a program needn't handle non-finite values.
Results may differ from the reference program's by a relative error of at most 0.0015.
Values may be sent and summed in bfloat16 or wider, within the bound.
A program may use at most 64 MiB of HBM per device.

```python
import math
import jax
import jax.numpy as jnp
from jax import lax

BLK = 128
ROWB_DEV = 4
COLB_DEV = 8
INST = 128
ITERS = 3
NZ_DEV = 48
NBLK = 768
ROWS = 8192
COLS = 16384
N_COL = 16


def block_pattern(base_key):
    device_count = NBLK // NZ_DEV
    slot_count = 3 * ROWB_DEV * COLB_DEV
    subkeys = jax.random.split(base_key, device_count)

    def one_device(subkey):
        shuffled = jax.random.permutation(subkey, slot_count)
        return jnp.sort(shuffled[:NZ_DEV])
    chosen = jax.vmap(one_device)(subkeys).astype(jnp.int32)
    owners = jnp.arange(device_count, dtype=jnp.int32)[:, None]
    row_index = jnp.mod((owners - 1) * ROWB_DEV + chosen // COLB_DEV, device_count * ROWB_DEV)
    col_index = owners * COLB_DEV + chosen % COLB_DEV
    return (row_index.reshape(-1).astype(jnp.int32), col_index.reshape(-1).astype(jnp.int32))


def draw_block_rows(key, part):
    shared = block_pattern(key)
    return shared[0]


def draw_block_cols(key, part):
    shared = block_pattern(key)
    return shared[1]


def plant(values, key, low, top_value):
    dims = values.shape
    spot = [jax.random.randint(jax.random.fold_in(key, axis), (), 0, dims[axis]) for axis in range(len(dims))]
    values = values.at[tuple(spot)].set(low)
    longest = dims.index(max(dims))
    spot[longest] = (spot[longest] + 1) % dims[longest]
    return values.at[tuple(spot)].set(top_value)


def level_of(own_key, shape, cuts, smallest, top_value):
    factor_of, own = 1.0, jax.random.fold_in(own_key, 6)
    for position, parts in cuts:
        steps = jnp.exp(jax.random.uniform(jax.random.fold_in(own, position), (parts,), jnp.float32, smallest / len(cuts), top_value / len(cuts)))
        factor_of = factor_of * jnp.repeat(steps, shape[position] // parts).reshape([-1 if axis == position else 1 for axis in range(len(shape))])
    return factor_of


def bell_draw(rng, shape, deviation, most, shards=(), kind=jnp.bfloat16):
    result = deviation * jax.random.normal(rng, shape, jnp.float32)
    if shards:
        result = result * level_of(rng, shape, shards, -0.22, 0.18)
    return jnp.clip(result, -most, most).astype(kind)


def setup_inputs(seed: int = 0, part: int = 0) -> dict:
    key_list = jax.random.split(jax.random.key(seed), 15)
    part_keys = jax.random.split(jax.random.fold_in(key_list[14], part), 15)
    blocks = bell_draw(key_list[0], (NBLK, BLK, BLK), (BLK * NZ_DEV // ROWB_DEV) ** -0.5, 0.15625, ((0, 16),))
    block_rows = draw_block_rows(jax.random.fold_in(key_list[14], 71), part)
    block_cols = draw_block_cols(jax.random.fold_in(key_list[14], 71), part)
    primal = bell_draw(part_keys[3], (COLS, INST), 0.5, 4.0, ((0, 16),), jnp.float32)
    dual = bell_draw(part_keys[4], (ROWS, INST), 0.5, 4.0, ((0, 16),), jnp.float32)
    anchor_primal = bell_draw(part_keys[5], (COLS, INST), 0.5, 4.0, ((0, 16),), jnp.float32)
    anchor_dual = bell_draw(part_keys[6], (ROWS, INST), 0.5, 4.0, ((0, 16),), jnp.float32)
    cost = bell_draw(part_keys[7], (COLS, INST), 1.0, 6.0, ((0, 16),), jnp.float32)
    rhs = bell_draw(part_keys[8], (ROWS, INST), 1.0, 6.0, ((0, 16),), jnp.float32)
    bound_kind = plant(jax.random.randint(part_keys[9], (COLS, INST), 0, 3), jax.random.fold_in(part_keys[9], 1), 0, 2).astype(jnp.int32)
    lower = jnp.clip(-1.5 + 1.3 * jax.random.uniform(key_list[10], (COLS,), jnp.float32) ** level_of(key_list[10], (COLS,), ((0, 16),), -0.2, 0.2), -1.5, -0.2)
    upper = jnp.clip(0.2 + 1.3 * jax.random.uniform(key_list[11], (COLS,), jnp.float32) ** level_of(key_list[11], (COLS,), ((0, 16),), -0.2, 0.2), 0.2, 1.5)
    step_size = jnp.clip(jnp.exp(jax.random.uniform(part_keys[12], (INST,), jnp.float32, math.log(0.1), math.log(0.4))), 0.1, 0.4)
    primal_weight = jnp.clip(jnp.exp(jax.random.uniform(part_keys[13], (INST,), jnp.float32, math.log(0.5), math.log(2.0))), 0.5, 2.0)
    return dict(blocks=blocks, block_rows=block_rows, block_cols=block_cols, primal=primal, dual=dual, anchor_primal=anchor_primal, anchor_dual=anchor_dual, cost=cost, rhs=rhs, bound_kind=bound_kind, lower=lower, upper=upper, step_size=step_size, primal_weight=primal_weight)


def project_bounds(values, bound_kind, lower, upper):
    low_side = lower[:, None]
    high_side = upper[:, None]
    lower_only = jnp.maximum(values, low_side)
    boxed = jnp.minimum(jnp.maximum(values, low_side), high_side)
    return jnp.where(bound_kind == 0, values, jnp.where(bound_kind == 1, lower_only, boxed))

def reference(blocks, block_rows, block_cols, primal, dual, anchor_primal, anchor_dual, cost, rhs, bound_kind, lower, upper, step_size, primal_weight):
    row_count = ROWS // BLK
    col_count = COLS // BLK
    grouped_blocks = blocks.reshape(N_COL, NZ_DEV, BLK, BLK)
    grouped_rows = block_rows.reshape(N_COL, NZ_DEV).astype(jnp.int32)
    grouped_cols = block_cols.reshape(N_COL, NZ_DEV).astype(jnp.int32)
    owners = jnp.arange(N_COL, dtype=jnp.int32)
    primal_step = step_size / primal_weight
    dual_step = step_size * primal_weight
    cells = jnp.float32(ROWS + COLS)
    current_x = primal
    current_y = dual
    residual_list = []
    for turn in range(ITERS):
        dual_rounded = current_y.astype(jnp.bfloat16).reshape(row_count, BLK, INST)

        def transpose_part(packed):
            part_blocks, part_rows, part_cols, owner = packed
            picked = dual_rounded[part_rows].astype(jnp.float32)
            products = jnp.einsum('kji,kjb->kib', part_blocks.astype(jnp.float32), picked)
            local_cols = (part_cols - owner * COLB_DEV).astype(jnp.int32)
            return jnp.zeros((COLB_DEV, BLK, INST), jnp.float32).at[local_cols].add(products)
        gradient = lax.map(transpose_part, (grouped_blocks, grouped_rows, grouped_cols, owners)).reshape(COLS, INST)
        primal_next = project_bounds(current_x - primal_step[None, :] * (cost - gradient), bound_kind, lower, upper)
        extrapolated = (2.0 * primal_next - current_x).astype(jnp.bfloat16).reshape(col_count, BLK, INST)

        def forward_part(total, packed):
            part_blocks, part_rows, part_cols = packed
            chosen = extrapolated[part_cols].astype(jnp.float32)
            products = jnp.einsum('kij,kjb->kib', part_blocks.astype(jnp.float32), chosen)
            return (total.at[part_rows].add(products), None)
        start_total = jnp.zeros((row_count, BLK, INST), jnp.float32)
        row_total, unused = lax.scan(forward_part, start_total, (grouped_blocks, grouped_rows, grouped_cols))
        row_products = row_total.reshape(ROWS, INST)
        dual_next = current_y + dual_step[None, :] * (rhs - row_products)
        primal_sq = lax.optimization_barrier(jnp.sum((primal_next - current_x) ** 2, axis=0))
        dual_sq = lax.optimization_barrier(jnp.sum((dual_next - current_y) ** 2, axis=0))
        residual_list.append(jnp.sqrt((primal_weight * primal_sq + dual_sq / primal_weight) / cells))
        mixing = (turn + 1.0) / (turn + 2.0)
        current_x = mixing * (2.0 * primal_next - current_x) + (1.0 - mixing) * anchor_primal
        current_y = mixing * (2.0 * dual_next - current_y) + (1.0 - mixing) * anchor_dual
    return (current_x, current_y, jnp.stack(residual_list))
```

```python
import functools

import jax
import jax.numpy as jnp
from jax import lax
from jax.experimental import pallas as pl
from jax.experimental.pallas import tpu as pltpu
from jax.sharding import PartitionSpec as P

ITERS = 3
CHUNKS = 2
FAR, NEAR, OWN = 0, 1, 2
MESH = pl.DeviceIdType.MESH


def kernel(
    n,
    blocks_hbm,
    rows_hbm,
    cols_hbm,
    primal_hbm,
    dual_hbm,
    anchor_primal_hbm,
    anchor_dual_hbm,
    cost_hbm,
    rhs_hbm,
    kind_hbm,
    lower_hbm,
    upper_hbm,
    step_hbm,
    weight_hbm,
    primal_out,
    dual_out,
    residual_out,
    blk,
    blk_t,
    rows,
    cols,
    table_v,
    table,
    mat,
    mat_t,
    x,
    x_next,
    anchor_x,
    cost,
    kind,
    low,
    high,
    low_rows,
    high_rows,
    grad,
    extra,
    y,
    anchor_y,
    rhs,
    own_y,
    halo,
    row_own,
    far_send,
    far_recv,
    near_send,
    near_recv,
    step,
    weight,
    res_send,
    res_recv,
    res,
    load_sem,
    store_sem,
    halo_send_sem,
    halo_recv_sem,
    part_send_sem,
    part_recv_sem,
    res_send_sem,
    res_recv_sem,
    table_sem,
):
    me = lax.axis_index("col")
    nz, size, _ = blocks_hbm.shape
    ncols, nrows = x.shape[0], y.shape[0]
    row_blocks, col_blocks = nrows // size, ncols // size
    part = nrows // CHUNKS
    parity = lax.rem(me, 2)
    far_dev = lax.rem(me + 2 * parity - 1 + n, n)
    near_dev = lax.rem(me + 1 - 2 * parity + n, n)
    partner = (far_dev, near_dev)

    barrier = pltpu.get_barrier_semaphore()

    def greet(k, carry):
        pl.semaphore_signal(barrier, inc=1, device_id={"col": lax.rem(me + k, n)}, device_id_type=MESH)
        return carry

    lax.fori_loop(1, n, greet, 0)

    loads = {}
    for place, (name, source, target) in enumerate(
        (
            ("y", dual_hbm, y),
            ("rows", rows_hbm, rows),
            ("cols", cols_hbm, cols),
            ("blocks", blocks_hbm, blk.at[pl.ds(1, nz)]),
            ("low", lower_hbm, low_rows),
            ("high", upper_hbm, high_rows),
            ("step", step_hbm, step),
            ("weight", weight_hbm, weight),
            ("x", primal_hbm, x),
            ("cost", cost_hbm, cost),
            ("kind", kind_hbm, kind),
            ("rhs", rhs_hbm, rhs),
            ("anchor_x", anchor_primal_hbm, anchor_x),
            ("anchor_y", anchor_dual_hbm, anchor_y),
        )
    ):
        loads[name] = pltpu.make_async_copy(source, target, load_sem.at[place])
        loads[name].start()

    def halo_copy(turn, who, c):
        return pltpu.make_async_remote_copy(
            src_ref=own_y.at[turn, c],
            dst_ref=halo.at[turn, who, c],
            send_sem=halo_send_sem.at[turn, who, c],
            recv_sem=halo_recv_sem.at[turn, who, c],
            device_id={"col": partner[who]},
            device_id_type=MESH,
        )

    part_send, part_recv = (far_send, near_send), (far_recv, near_recv)

    def part_copy(turn, who, c):
        return pltpu.make_async_remote_copy(
            src_ref=part_send[who].at[turn, c],
            dst_ref=part_recv[who].at[turn, c],
            send_sem=part_send_sem.at[turn, who, c],
            recv_sem=part_recv_sem.at[turn, who, c],
            device_id={"col": partner[who]},
            device_id_type=MESH,
        )

    sent = []
    loads["y"].wait()
    for c in range(CHUNKS):
        own_y[0, c] = y[c * part : (c + 1) * part].astype(jnp.bfloat16)
    pl.semaphore_wait(barrier, n - 1)
    for c in range(CHUNKS):
        for who in (FAR, NEAR):
            copy = halo_copy(0, who, c)
            copy.start()
            sent.append(copy)

    loads["rows"].wait()
    loads["cols"].wait()
    local_row = rows[...] - (me - 1) * row_blocks
    local_row = jnp.where(local_row < 0, local_row + row_blocks * n, local_row)
    local_row = jnp.where(local_row >= row_blocks * n, local_row - row_blocks * n, local_row)
    segment = jnp.where(local_row >= 2 * row_blocks, 2, jnp.where(local_row >= row_blocks, 1, 0))
    owner = jnp.where(segment == 1, OWN, jnp.where(segment == 2 * parity, FAR, NEAR))
    band_row = local_row + (owner - segment) * row_blocks
    place = band_row * col_blocks + cols[...] - me * col_blocks
    match = lax.broadcasted_iota(jnp.int32, (128, nz), 0) == place
    number = lax.broadcasted_iota(jnp.int32, (128, nz), 1) + 1
    found = jnp.max(jnp.where(match, number, 0), axis=1, keepdims=True)
    table_v[...] = jnp.transpose(jnp.broadcast_to(found, (128, 128)))[0:1]
    to_scalar = pltpu.make_async_copy(table_v, table, table_sem)
    to_scalar.start()

    loads["low"].wait()
    loads["high"].wait()
    for c in range(col_blocks):
        span = slice(c * size, (c + 1) * size)
        low[span] = jnp.transpose(jnp.broadcast_to(low_rows[c : c + 1], (size, x.shape[1])))
        high[span] = jnp.transpose(jnp.broadcast_to(high_rows[c : c + 1], (size, x.shape[1])))

    blk[0] = jnp.zeros((size, size), jnp.bfloat16)
    blk_t[0] = jnp.zeros((size, size), jnp.bfloat16)
    loads["blocks"].wait()

    def turn_block(k, carry):
        blk_t[k] = jnp.transpose(blk[k])
        return carry

    lax.fori_loop(1, nz + 1, turn_block, 0, unroll=4)
    to_scalar.wait()

    def build(r, carry):
        down = pl.ds(pl.multiple_of(r * size, size), size)
        for c in range(col_blocks):
            which = table[0, r * col_blocks + c]
            mat[down, c * size : (c + 1) * size] = blk[which]
            mat_t[c * size : (c + 1) * size, down] = blk_t[which]
        return carry

    lax.fori_loop(0, 3 * row_blocks, build, 0)

    loads["step"].wait()
    loads["weight"].wait()
    primal_step = step[...] / weight[...]
    dual_step = step[...] * weight[...]
    res_send[...] = jnp.zeros_like(res_send)
    for name in ("x", "cost", "kind"):
        loads[name].wait()

    def times(left, right):
        return jnp.dot(left, right, preferred_element_type=jnp.float32)

    width = 256
    for turn in range(ITERS):
        first = {FAR: 0, NEAR: nrows, OWN: 2 * nrows}
        grad[...] = times(
            mat_t[:, 2 * nrows : 3 * nrows],
            jnp.concatenate([own_y[turn, c] for c in range(CHUNKS)], axis=0),
        )
        order = [(NEAR, c) for c in range(CHUNKS)] + [(FAR, c) for c in range(CHUNKS)]
        for who, c in order[:-1]:
            halo_copy(turn, who, c).wait_recv()
            at = first[who] + c * part
            grad[...] += times(mat_t[:, at : at + part], halo[turn, who, c])
        who, c = order[-1]
        halo_copy(turn, who, c).wait_recv()
        at = first[who] + c * part
        for i in range(0, ncols, width):
            span = slice(i, i + width)
            total = grad[span] + times(mat_t[span, at : at + part], halo[turn, who, c])
            now = x[span]
            value = now - primal_step * (cost[span] - total)
            of_kind = kind[span]
            lower_only = jnp.maximum(value, low[span])
            boxed = jnp.minimum(lower_only, high[span])
            after = jnp.where(of_kind == 0, value, jnp.where(of_kind == 1, lower_only, boxed))
            x_next[span] = after
            extra[span] = (2.0 * after - now).astype(jnp.bfloat16)

        for who in (FAR, NEAR):
            for c in range(CHUNKS):
                at = first[who] + c * part
                part_send[who][turn, c] = times(mat[at : at + part], extra[...]).astype(part_send[who].dtype)
                copy = part_copy(turn, who, c)
                copy.start()
                sent.append(copy)
        row_own[...] = times(mat[2 * nrows :], extra[...])

        mixing = (turn + 1.0) / (turn + 2.0)
        if turn == 0:
            loads["anchor_x"].wait()
        primal_sq = jnp.zeros((1, x.shape[1]), jnp.float32)
        for i in range(0, ncols, width):
            span = slice(i, i + width)
            now, after = x[span], x_next[span]
            primal_sq += jnp.sum((after - now) ** 2, axis=0, keepdims=True)
            x[span] = mixing * (2.0 * after - now) + (1.0 - mixing) * anchor_x[span]
        if turn == ITERS - 1:
            x_store = pltpu.make_async_copy(x, primal_out, store_sem.at[0])
            x_store.start()

        if turn == 0:
            loads["rhs"].wait()
            loads["anchor_y"].wait()
        dual_sq = jnp.zeros((1, x.shape[1]), jnp.float32)
        for c in range(CHUNKS):
            span = slice(c * part, (c + 1) * part)
            part_copy(turn, NEAR, c).wait_recv()
            part_copy(turn, FAR, c).wait_recv()
            products = (
                row_own[span]
                + near_recv[turn, c]
                + far_recv[turn, c].astype(jnp.float32)
            )
            now = y[span]
            after = now + dual_step * (rhs[span] - products)
            new = mixing * (2.0 * after - now) + (1.0 - mixing) * anchor_y[span]
            y[span] = new
            if turn < ITERS - 1:
                own_y[turn + 1, c] = new.astype(jnp.bfloat16)
                for who in (FAR, NEAR):
                    copy = halo_copy(turn + 1, who, c)
                    copy.start()
                    sent.append(copy)
            dual_sq += jnp.sum((after - now) ** 2, axis=0, keepdims=True)
        res_send[turn : turn + 1] = weight[...] * primal_sq + dual_sq / weight[...]

    def res_copy(k):
        return pltpu.make_async_remote_copy(
            src_ref=res_send,
            dst_ref=res_recv.at[k],
            send_sem=res_send_sem.at[k],
            recv_sem=res_recv_sem.at[k],
            device_id={"col": lax.rem(me + k, n)},
            device_id_type=MESH,
        )

    def spread(k, carry):
        res_copy(k).start()
        return carry

    lax.fori_loop(1, n, spread, 0)
    y_store = pltpu.make_async_copy(y, dual_out, store_sem.at[1])
    y_store.start()
    res_recv[0] = res_send[...]
    for copy in sent:
        copy.wait_send()

    def collect(k, carry):
        res_copy(k).wait()
        return carry

    lax.fori_loop(1, n, collect, 0)
    total = jnp.sum(res_recv[...], axis=0)
    cells = jnp.float32((ncols + nrows) * n)
    res[...] = jnp.sqrt(total[0:ITERS] / cells)
    res_store = pltpu.make_async_copy(res, residual_out, store_sem.at[2])
    res_store.start()
    x_store.wait()
    y_store.wait()
    res_store.wait()


def per_device(
    blocks,
    block_rows,
    block_cols,
    primal,
    dual,
    anchor_primal,
    anchor_dual,
    cost,
    rhs,
    bound_kind,
    lower,
    upper,
    step_size,
    primal_weight,
):
    n = lax.axis_size("col")
    nz, size, _ = blocks.shape
    ncols, inst = primal.shape
    nrows = dual.shape[0]
    part = nrows // CHUNKS
    f32, bf16, i32 = jnp.float32, jnp.bfloat16, jnp.int32
    any_space = pl.BlockSpec(memory_space=pl.ANY)
    vmem = pltpu.VMEM
    dma = pltpu.SemaphoreType.DMA
    return pl.pallas_call(
        functools.partial(kernel, n),
        out_shape=(
            jax.ShapeDtypeStruct((ncols, inst), f32),
            jax.ShapeDtypeStruct((nrows, inst), f32),
            jax.ShapeDtypeStruct((ITERS, inst), f32),
        ),
        in_specs=[any_space] * 14,
        out_specs=(any_space,) * 3,
        scratch_shapes=[
            vmem((nz + 1, size, size), bf16),
            vmem((nz + 1, size, size), bf16),
            vmem((1, nz), i32),
            vmem((1, nz), i32),
            vmem((1, 128), i32),
            pltpu.SMEM((1, 128), i32),
            vmem((3 * nrows, ncols), bf16),
            vmem((ncols, 3 * nrows), bf16),
            vmem((ncols, inst), f32),
            vmem((ncols, inst), f32),
            vmem((ncols, inst), f32),
            vmem((ncols, inst), f32),
            vmem((ncols, inst), i32),
            vmem((ncols, inst), f32),
            vmem((ncols, inst), f32),
            vmem((ncols // size, size), f32),
            vmem((ncols // size, size), f32),
            vmem((ncols, inst), f32),
            vmem((ncols, inst), bf16),
            vmem((nrows, inst), f32),
            vmem((nrows, inst), f32),
            vmem((nrows, inst), f32),
            vmem((ITERS, CHUNKS, part, inst), bf16),
            vmem((ITERS, 2, CHUNKS, part, inst), bf16),
            vmem((nrows, inst), f32),
            vmem((ITERS, CHUNKS, part, inst), bf16),
            vmem((ITERS, CHUNKS, part, inst), bf16),
            vmem((ITERS, CHUNKS, part, inst), f32),
            vmem((ITERS, CHUNKS, part, inst), f32),
            vmem((1, inst), f32),
            vmem((1, inst), f32),
            vmem((8, inst), f32),
            vmem((n, 8, inst), f32),
            vmem((ITERS, inst), f32),
            dma((14,)),
            dma((3,)),
            dma((ITERS, 2, CHUNKS)),
            dma((ITERS, 2, CHUNKS)),
            dma((ITERS, 2, CHUNKS)),
            dma((ITERS, 2, CHUNKS)),
            dma((n,)),
            dma((n,)),
            dma,
        ],
        compiler_params=pltpu.CompilerParams(
            collective_id=0, has_side_effects=True, vmem_limit_bytes=56 * 1024 * 1024
        ),
        cost_estimate=pl.CostEstimate(
            flops=4 * ITERS * nz * size * size * inst, bytes_accessed=6 * 2**20, transcendentals=0
        ),
    )(
        blocks,
        block_rows.reshape(1, nz),
        block_cols.reshape(1, nz),
        primal,
        dual,
        anchor_primal,
        anchor_dual,
        cost,
        rhs,
        bound_kind,
        lower.reshape(ncols // size, size),
        upper.reshape(ncols // size, size),
        step_size.reshape(1, inst),
        primal_weight.reshape(1, inst),
    )


def solution(mesh):
    return jax.shard_map(
        per_device,
        mesh=mesh,
        in_specs=(
            P("col", None, None),
            P("col"),
            P("col"),
            P("col", "groups"),
            P("col", "groups"),
            P("col", "groups"),
            P("col", "groups"),
            P("col", "groups"),
            P("col", "groups"),
            P("col", "groups"),
            P("col"),
            P("col"),
            P("groups"),
            P("groups"),
        ),
        out_specs=(P("col", "groups"), P("col", "groups"), P(None, "groups")),
        check_vma=False,
    )
```

```python
import functools

import jax
import jax.numpy as jnp
from jax import lax
from jax.experimental import pallas as pl
from jax.experimental.pallas import tpu as pltpu
from jax.sharding import PartitionSpec as P

ITERS = 3
CHUNKS = 2
FAR, NEAR, OWN = 0, 1, 2
MESH = pl.DeviceIdType.MESH


def kernel(
    n,
    blocks_hbm,
    rows_hbm,
    cols_hbm,
    primal_hbm,
    dual_hbm,
    anchor_primal_hbm,
    anchor_dual_hbm,
    cost_hbm,
    rhs_hbm,
    kind_hbm,
    lower_hbm,
    upper_hbm,
    step_hbm,
    weight_hbm,
    primal_out,
    dual_out,
    residual_out,
    blk,
    blk_t,
    rows,
    cols,
    table_v,
    table,
    mat,
    mat_t,
    x_next,
    anchor_x,
    cost,
    kind,
    low,
    high,
    low_rows,
    high_rows,
    grad,
    extra,
    base,
    anchor_y,
    rhs,
    own_y,
    halo,
    row_own,
    far_send,
    far_recv,
    near_send,
    near_recv,
    step,
    weight,
    res_send,
    res_recv,
    load_sem,
    halo_send_sem,
    halo_recv_sem,
    part_send_sem,
    part_recv_sem,
    res_send_sem,
    res_recv_sem,
    table_sem,
):
    x, y = primal_out, dual_out
    me = lax.axis_index("col")
    nz, size, _ = blocks_hbm.shape
    ncols, nrows = x.shape[0], y.shape[0]
    row_blocks, col_blocks = nrows // size, ncols // size
    part = nrows // CHUNKS
    parity = lax.rem(me, 2)
    far_dev = lax.rem(me + 2 * parity - 1 + n, n)
    near_dev = lax.rem(me + 1 - 2 * parity + n, n)
    partner = (far_dev, near_dev)

    barrier = pltpu.get_barrier_semaphore()

    def greet(k, carry):
        pl.semaphore_signal(barrier, inc=1, device_id={"col": lax.rem(me + k, n)}, device_id_type=MESH)
        return carry

    lax.fori_loop(1, n, greet, 0)

    loads = {}
    for place, (name, source, target) in enumerate(
        (
            ("rows", rows_hbm, rows),
            ("cols", cols_hbm, cols),
            ("y", dual_hbm, y),
            ("blocks", blocks_hbm, blk.at[pl.ds(1, nz)]),
            ("low", lower_hbm, low_rows),
            ("high", upper_hbm, high_rows),
            ("step", step_hbm, step),
            ("weight", weight_hbm, weight),
            ("x", primal_hbm, x),
            ("cost", cost_hbm, cost),
            ("kind", kind_hbm, kind),
            ("rhs", rhs_hbm, rhs),
            ("anchor_x", anchor_primal_hbm, anchor_x),
            ("anchor_y", anchor_dual_hbm, anchor_y),
        )
    ):
        loads[name] = pltpu.make_async_copy(source, target, load_sem.at[place])
        loads[name].start()

    def halo_copy(turn, who, c):
        return pltpu.make_async_remote_copy(
            src_ref=own_y.at[turn, c],
            dst_ref=halo.at[turn, who, c],
            send_sem=halo_send_sem.at[turn, who, c],
            recv_sem=halo_recv_sem.at[turn, who, c],
            device_id={"col": partner[who]},
            device_id_type=MESH,
        )

    part_send, part_recv = (far_send, near_send), (far_recv, near_recv)

    def part_copy(turn, who, c):
        return pltpu.make_async_remote_copy(
            src_ref=part_send[who].at[turn, c],
            dst_ref=part_recv[who].at[turn, c],
            send_sem=part_send_sem.at[turn, who, c],
            recv_sem=part_recv_sem.at[turn, who, c],
            device_id={"col": partner[who]},
            device_id_type=MESH,
        )

    loads["rows"].wait()
    loads["cols"].wait()
    local_row = rows[...] - (me - 1) * row_blocks
    local_row = jnp.where(local_row < 0, local_row + row_blocks * n, local_row)
    local_row = jnp.where(local_row >= row_blocks * n, local_row - row_blocks * n, local_row)
    segment = jnp.where(local_row >= 2 * row_blocks, 2, jnp.where(local_row >= row_blocks, 1, 0))
    owner = jnp.where(segment == 1, OWN, jnp.where(segment == 2 * parity, FAR, NEAR))
    band_row = local_row + (owner - segment) * row_blocks
    place = band_row * col_blocks + cols[...] - me * col_blocks
    match = lax.broadcasted_iota(jnp.int32, (128, nz), 0) == place
    number = lax.broadcasted_iota(jnp.int32, (128, nz), 1) + 1
    found = jnp.max(jnp.where(match, number, 0), axis=1, keepdims=True)
    table_v[...] = jnp.transpose(jnp.broadcast_to(found, (128, 128)))[0:1]
    to_scalar = pltpu.make_async_copy(table_v, table, table_sem)
    to_scalar.start()

    sent = []
    loads["y"].wait()
    for c in range(CHUNKS):
        own_y[0, c] = y[c * part : (c + 1) * part].astype(jnp.bfloat16)
    pl.semaphore_wait(barrier, n - 1)
    for c in range(CHUNKS):
        for who in (FAR, NEAR):
            copy = halo_copy(0, who, c)
            copy.start()
            sent.append(copy)

    blk[0] = jnp.zeros((size, size), jnp.bfloat16)
    blk_t[0] = jnp.zeros((size, size), jnp.bfloat16)
    loads["blocks"].wait()

    def turn_block(k, carry):
        blk_t[k] = jnp.transpose(blk[k])
        return carry

    lax.fori_loop(1, nz + 1, turn_block, 0, unroll=4)
    to_scalar.wait()

    def build(r, carry):
        down = pl.ds(pl.multiple_of(r * size, size), size)
        for c in range(col_blocks):
            which = table[0, r * col_blocks + c]
            mat[down, c * size : (c + 1) * size] = blk[which]
            mat_t[c * size : (c + 1) * size, down] = blk_t[which]
        return carry

    lax.fori_loop(0, 3 * row_blocks, build, 0)

    loads["step"].wait()
    loads["weight"].wait()
    primal_step = step[...] / weight[...]
    dual_step = step[...] * weight[...]
    for name in ("low", "high", "kind", "x", "cost"):
        loads[name].wait()
    for c in range(col_blocks):
        span = slice(c * size, (c + 1) * size)
        of_kind = kind[span]
        low_side = jnp.transpose(jnp.broadcast_to(low_rows[c : c + 1], (size, x.shape[1])))
        high_side = jnp.transpose(jnp.broadcast_to(high_rows[c : c + 1], (size, x.shape[1])))
        low[span] = jnp.where(of_kind == 0, -jnp.inf, low_side)
        high[span] = jnp.where(of_kind == 2, high_side, jnp.inf)
        base[span] = x[span] - primal_step * cost[span]

    def times(left, right):
        return jnp.dot(left, right, preferred_element_type=jnp.float32)

    width = 256
    for turn in range(ITERS):
        first = {FAR: 0, NEAR: nrows, OWN: 2 * nrows}
        grad[...] = times(
            mat_t[:, 2 * nrows : 3 * nrows],
            jnp.concatenate([own_y[turn, c] for c in range(CHUNKS)], axis=0),
        )
        order = [(NEAR, c) for c in range(CHUNKS)] + [(FAR, c) for c in range(CHUNKS)]
        for who, c in order[:-1]:
            halo_copy(turn, who, c).wait_recv()
            at = first[who] + c * part
            grad[...] += times(mat_t[:, at : at + part], halo[turn, who, c])
        who, c = order[-1]
        halo_copy(turn, who, c).wait_recv()
        at = first[who] + c * part
        for i in range(0, ncols, width):
            span = slice(i, i + width)
            total = grad[span] + times(mat_t[span, at : at + part], halo[turn, who, c])
            value = base[span] + primal_step * total
            after = jnp.minimum(jnp.maximum(value, low[span]), high[span])
            x_next[span] = after
            extra[span] = (2.0 * after - x[span]).astype(jnp.bfloat16)

        for who in (FAR, NEAR):
            for c in range(CHUNKS):
                at = first[who] + c * part
                part_send[who][turn, c] = times(mat[at : at + part], extra[...]).astype(part_send[who].dtype)
                copy = part_copy(turn, who, c)
                copy.start()
                sent.append(copy)
        row_own[...] = times(mat[2 * nrows :], extra[...])

        mixing = (turn + 1.0) / (turn + 2.0)
        if turn == 0:
            loads["anchor_x"].wait()
        primal_sq = jnp.zeros((1, x.shape[1]), jnp.float32)
        for i in range(0, ncols, width):
            span = slice(i, i + width)
            now, after = x[span], x_next[span]
            primal_sq += jnp.sum((after - now) ** 2, axis=0, keepdims=True)
            new = mixing * (2.0 * after - now) + (1.0 - mixing) * anchor_x[span]
            x[span] = new
            if turn < ITERS - 1:
                base[span] = new - primal_step * cost[span]

        if turn == 0:
            loads["rhs"].wait()
            loads["anchor_y"].wait()
        dual_sq = jnp.zeros((1, x.shape[1]), jnp.float32)
        for c in range(CHUNKS):
            span = slice(c * part, (c + 1) * part)
            part_copy(turn, NEAR, c).wait_recv()
            part_copy(turn, FAR, c).wait_recv()
            products = (
                row_own[span]
                + near_recv[turn, c]
                + far_recv[turn, c].astype(jnp.float32)
            )
            now = y[span]
            after = now + dual_step * (rhs[span] - products)
            new = mixing * (2.0 * after - now) + (1.0 - mixing) * anchor_y[span]
            y[span] = new
            if turn < ITERS - 1:
                own_y[turn + 1, c] = new.astype(jnp.bfloat16)
                for who in (FAR, NEAR):
                    copy = halo_copy(turn + 1, who, c)
                    copy.start()
                    sent.append(copy)
            dual_sq += jnp.sum((after - now) ** 2, axis=0, keepdims=True)
        res_send[turn : turn + 1] = weight[...] * primal_sq + dual_sq / weight[...]

    def res_copy(k):
        return pltpu.make_async_remote_copy(
            src_ref=res_send,
            dst_ref=res_recv.at[k],
            send_sem=res_send_sem.at[k],
            recv_sem=res_recv_sem.at[k],
            device_id={"col": lax.rem(me + k, n)},
            device_id_type=MESH,
        )

    def spread(k, carry):
        res_copy(k).start()
        return carry

    lax.fori_loop(1, n, spread, 0)
    res_recv[0] = res_send[...]
    for copy in sent:
        copy.wait_send()

    def collect(k, carry):
        res_copy(k).wait()
        return carry

    lax.fori_loop(1, n, collect, 0)
    total = jnp.sum(res_recv[...], axis=0)
    cells = jnp.float32((ncols + nrows) * n)
    residual_out[...] = jnp.sqrt(total / cells)


def per_device(
    blocks,
    block_rows,
    block_cols,
    primal,
    dual,
    anchor_primal,
    anchor_dual,
    cost,
    rhs,
    bound_kind,
    lower,
    upper,
    step_size,
    primal_weight,
):
    n = lax.axis_size("col")
    nz, size, _ = blocks.shape
    ncols, inst = primal.shape
    nrows = dual.shape[0]
    part = nrows // CHUNKS
    f32, bf16, i32 = jnp.float32, jnp.bfloat16, jnp.int32
    any_space = pl.BlockSpec(memory_space=pl.ANY)
    vmem = pltpu.VMEM
    dma = pltpu.SemaphoreType.DMA
    return pl.pallas_call(
        functools.partial(kernel, n),
        out_shape=(
            vmem((ncols, inst), f32),
            vmem((nrows, inst), f32),
            vmem((ITERS, inst), f32),
        ),
        in_specs=[any_space] * 14,
        out_specs=(pl.BlockSpec(memory_space=vmem),) * 3,
        scratch_shapes=[
            vmem((nz + 1, size, size), bf16),
            vmem((nz + 1, size, size), bf16),
            vmem((1, nz), i32),
            vmem((1, nz), i32),
            vmem((1, 128), i32),
            pltpu.SMEM((1, 128), i32),
            vmem((3 * nrows, ncols), bf16),
            vmem((ncols, 3 * nrows), bf16),
            vmem((ncols, inst), f32),
            vmem((ncols, inst), f32),
            vmem((ncols, inst), f32),
            vmem((ncols, inst), i32),
            vmem((ncols, inst), f32),
            vmem((ncols, inst), f32),
            vmem((ncols // size, size), f32),
            vmem((ncols // size, size), f32),
            vmem((ncols, inst), f32),
            vmem((ncols, inst), bf16),
            vmem((ncols, inst), f32),
            vmem((nrows, inst), f32),
            vmem((nrows, inst), f32),
            vmem((ITERS, CHUNKS, part, inst), bf16),
            vmem((ITERS, 2, CHUNKS, part, inst), bf16),
            vmem((nrows, inst), f32),
            vmem((ITERS, CHUNKS, part, inst), bf16),
            vmem((ITERS, CHUNKS, part, inst), bf16),
            vmem((ITERS, CHUNKS, part, inst), f32),
            vmem((ITERS, CHUNKS, part, inst), f32),
            vmem((1, inst), f32),
            vmem((1, inst), f32),
            vmem((ITERS, inst), f32),
            vmem((n, ITERS, inst), f32),
            dma((14,)),
            dma((ITERS, 2, CHUNKS)),
            dma((ITERS, 2, CHUNKS)),
            dma((ITERS, 2, CHUNKS)),
            dma((ITERS, 2, CHUNKS)),
            dma((n,)),
            dma((n,)),
            dma,
        ],
        compiler_params=pltpu.CompilerParams(
            collective_id=0, has_side_effects=True, vmem_limit_bytes=56 * 1024 * 1024
        ),
        cost_estimate=pl.CostEstimate(
            flops=4 * ITERS * nz * size * size * inst, bytes_accessed=6 * 2**20, transcendentals=0
        ),
    )(
        blocks,
        block_rows.reshape(1, nz),
        block_cols.reshape(1, nz),
        primal,
        dual,
        anchor_primal,
        anchor_dual,
        cost,
        rhs,
        bound_kind,
        lower.reshape(ncols // size, size),
        upper.reshape(ncols // size, size),
        step_size.reshape(1, inst),
        primal_weight.reshape(1, inst),
    )


def solution(mesh):
    return jax.shard_map(
        per_device,
        mesh=mesh,
        in_specs=(
            P("col", None, None),
            P("col"),
            P("col"),
            P("col", "groups"),
            P("col", "groups"),
            P("col", "groups"),
            P("col", "groups"),
            P("col", "groups"),
            P("col", "groups"),
            P("col", "groups"),
            P("col"),
            P("col"),
            P("groups"),
            P("groups"),
        ),
        out_specs=(P("col", "groups"), P("col", "groups"), P(None, "groups")),
        check_vma=False,
    )
```

```python
import functools

import jax
import jax.numpy as jnp
from jax import lax
from jax.experimental import pallas as pl
from jax.experimental.pallas import tpu as pltpu
from jax.sharding import PartitionSpec as P

ITERS = 3
CHUNKS = 2
FAR, NEAR, OWN = 0, 1, 2
MESH = pl.DeviceIdType.MESH


def kernel(
    n,
    blocks_hbm,
    rows_hbm,
    cols_hbm,
    primal_hbm,
    dual_hbm,
    anchor_primal_hbm,
    anchor_dual_hbm,
    cost_hbm,
    rhs_hbm,
    kind_hbm,
    lower_hbm,
    upper_hbm,
    step_hbm,
    weight_hbm,
    primal_out,
    dual_out,
    residual_out,
    blk,
    blk_t,
    rows,
    cols,
    table_v,
    table,
    mat,
    mat_t,
    x_next,
    anchor_x,
    cost,
    kind,
    low,
    high,
    low_rows,
    high_rows,
    grad,
    extra,
    base,
    anchor_y,
    rhs,
    own_y,
    halo,
    row_own,
    far_send,
    far_recv,
    near_send,
    near_recv,
    step,
    weight,
    res_send,
    res_recv,
    load_sem,
    halo_send_sem,
    halo_recv_sem,
    part_send_sem,
    part_recv_sem,
    res_send_sem,
    res_recv_sem,
    table_sem,
):
    x, y = primal_out, dual_out
    me = lax.axis_index("col")
    nz, size, _ = blocks_hbm.shape
    ncols, nrows = x.shape[0], y.shape[0]
    row_blocks, col_blocks = nrows // size, ncols // size
    part = nrows // CHUNKS
    parity = lax.rem(me, 2)
    far_dev = lax.rem(me + 2 * parity - 1 + n, n)
    near_dev = lax.rem(me + 1 - 2 * parity + n, n)
    partner = (far_dev, near_dev)

    barrier = pltpu.get_barrier_semaphore()

    def greet(k, carry):
        pl.semaphore_signal(barrier, inc=1, device_id={"col": lax.rem(me + k, n)}, device_id_type=MESH)
        return carry

    lax.fori_loop(1, n, greet, 0)

    loads = {}
    for place, (name, source, target) in enumerate(
        (
            ("rows", rows_hbm, rows),
            ("cols", cols_hbm, cols),
            ("y", dual_hbm, y),
            ("blocks", blocks_hbm, blk.at[pl.ds(1, nz)]),
            ("low", lower_hbm, low_rows),
            ("high", upper_hbm, high_rows),
            ("step", step_hbm, step),
            ("weight", weight_hbm, weight),
            ("x", primal_hbm, x),
            ("cost", cost_hbm, cost),
            ("kind", kind_hbm, kind),
            ("rhs", rhs_hbm, rhs),
            ("anchor_x", anchor_primal_hbm, anchor_x),
            ("anchor_y", anchor_dual_hbm, anchor_y),
        )
    ):
        loads[name] = pltpu.make_async_copy(source, target, load_sem.at[place])
        loads[name].start()

    def halo_copy(turn, who, c):
        return pltpu.make_async_remote_copy(
            src_ref=own_y.at[turn, c],
            dst_ref=halo.at[turn, who, c],
            send_sem=halo_send_sem.at[turn, who, c],
            recv_sem=halo_recv_sem.at[turn, who, c],
            device_id={"col": partner[who]},
            device_id_type=MESH,
        )

    part_send, part_recv = (far_send, near_send), (far_recv, near_recv)

    def part_copy(turn, who, c):
        return pltpu.make_async_remote_copy(
            src_ref=part_send[who].at[turn, c],
            dst_ref=part_recv[who].at[turn, c],
            send_sem=part_send_sem.at[turn, who, c],
            recv_sem=part_recv_sem.at[turn, who, c],
            device_id={"col": partner[who]},
            device_id_type=MESH,
        )

    loads["rows"].wait()
    loads["cols"].wait()
    local_row = rows[...] - (me - 1) * row_blocks
    local_row = jnp.where(local_row < 0, local_row + row_blocks * n, local_row)
    local_row = jnp.where(local_row >= row_blocks * n, local_row - row_blocks * n, local_row)
    segment = jnp.where(local_row >= 2 * row_blocks, 2, jnp.where(local_row >= row_blocks, 1, 0))
    owner = jnp.where(segment == 1, OWN, jnp.where(segment == 2 * parity, FAR, NEAR))
    band_row = local_row + (owner - segment) * row_blocks
    place = band_row * col_blocks + cols[...] - me * col_blocks
    match = lax.broadcasted_iota(jnp.int32, (128, nz), 0) == place
    number = lax.broadcasted_iota(jnp.int32, (128, nz), 1) + 1
    found = jnp.max(jnp.where(match, number, 0), axis=1, keepdims=True)
    table_v[...] = jnp.transpose(jnp.broadcast_to(found, (128, 128)))[0:1]
    to_scalar = pltpu.make_async_copy(table_v, table, table_sem)
    to_scalar.start()

    sent = []
    loads["y"].wait()
    for c in range(CHUNKS):
        own_y[0, c] = y[c * part : (c + 1) * part].astype(jnp.bfloat16)
    pl.semaphore_wait(barrier, n - 1)
    for c in range(CHUNKS):
        for who in (FAR, NEAR):
            copy = halo_copy(0, who, c)
            copy.start()
            sent.append(copy)

    blk[0] = jnp.zeros((size, size), jnp.bfloat16)
    blk_t[0] = jnp.zeros((size, size), jnp.bfloat16)
    loads["blocks"].wait()

    def turn_block(k, carry):
        blk_t[k] = jnp.transpose(blk[k])
        return carry

    lax.fori_loop(1, nz + 1, turn_block, 0, unroll=4)
    to_scalar.wait()

    def build(r, carry):
        down = pl.ds(pl.multiple_of(r * size, size), size)
        for c in range(col_blocks):
            which = table[0, r * col_blocks + c]
            mat[down, c * size : (c + 1) * size] = blk[which]
            mat_t[c * size : (c + 1) * size, down] = blk_t[which]
        return carry

    lax.fori_loop(0, 3 * row_blocks, build, 0)

    loads["step"].wait()
    loads["weight"].wait()
    primal_step = step[...] / weight[...]
    dual_step = step[...] * weight[...]
    for name in ("low", "high", "kind", "x", "cost"):
        loads[name].wait()
    for c in range(col_blocks):
        span = slice(c * size, (c + 1) * size)
        of_kind = kind[span]
        low_side = jnp.transpose(jnp.broadcast_to(low_rows[c : c + 1], (size, x.shape[1])))
        high_side = jnp.transpose(jnp.broadcast_to(high_rows[c : c + 1], (size, x.shape[1])))
        low[span] = jnp.where(of_kind == 0, -jnp.inf, low_side)
        high[span] = jnp.where(of_kind == 2, high_side, jnp.inf)
        base[span] = x[span] - primal_step * cost[span]

    def times(left, right):
        return jnp.dot(left, right, preferred_element_type=jnp.float32)

    width = 256
    for turn in range(ITERS):
        first = {FAR: 0, NEAR: nrows, OWN: 2 * nrows}
        grad[...] = times(
            mat_t[:, 2 * nrows : 3 * nrows],
            jnp.concatenate([own_y[turn, c] for c in range(CHUNKS)], axis=0),
        )
        order = [(NEAR, c) for c in range(CHUNKS)] + [(FAR, c) for c in range(CHUNKS)]
        for who, c in order[:-1]:
            halo_copy(turn, who, c).wait_recv()
            at = first[who] + c * part
            grad[...] += times(mat_t[:, at : at + part], halo[turn, who, c])
        who, c = order[-1]
        halo_copy(turn, who, c).wait_recv()
        at = first[who] + c * part
        for i in range(0, ncols, width):
            span = slice(i, i + width)
            total = grad[span] + times(mat_t[span, at : at + part], halo[turn, who, c])
            value = base[span] + primal_step * total
            after = jnp.minimum(jnp.maximum(value, low[span]), high[span])
            x_next[span] = after
            extra[span] = (2.0 * after - x[span]).astype(jnp.bfloat16)

        for who in (FAR, NEAR):
            for c in range(CHUNKS):
                at = first[who] + c * part
                part_send[who][turn, c] = times(mat[at : at + part], extra[...]).astype(part_send[who].dtype)
                copy = part_copy(turn, who, c)
                copy.start()
                sent.append(copy)
        row_own[...] = times(mat[2 * nrows :], extra[...])

        mixing = (turn + 1.0) / (turn + 2.0)
        if turn == 0:
            loads["anchor_x"].wait()
        primal_sq = jnp.zeros((1, x.shape[1]), jnp.float32)
        for i in range(0, ncols, width):
            span = slice(i, i + width)
            now, after = x[span], x_next[span]
            primal_sq += jnp.sum((after - now) ** 2, axis=0, keepdims=True)
            new = mixing * (2.0 * after - now) + (1.0 - mixing) * anchor_x[span]
            x[span] = new
            if turn < ITERS - 1:
                base[span] = new - primal_step * cost[span]

        if turn == 0:
            loads["rhs"].wait()
            loads["anchor_y"].wait()
        dual_sq = jnp.zeros((1, x.shape[1]), jnp.float32)
        for c in range(CHUNKS):
            span = slice(c * part, (c + 1) * part)
            part_copy(turn, NEAR, c).wait_recv()
            part_copy(turn, FAR, c).wait_recv()
            products = (
                row_own[span]
                + near_recv[turn, c]
                + far_recv[turn, c].astype(jnp.float32)
            )
            now = y[span]
            after = now + dual_step * (rhs[span] - products)
            new = mixing * (2.0 * after - now) + (1.0 - mixing) * anchor_y[span]
            y[span] = new
            if turn < ITERS - 1:
                own_y[turn + 1, c] = new.astype(jnp.bfloat16)
                for who in (FAR, NEAR):
                    copy = halo_copy(turn + 1, who, c)
                    copy.start()
                    sent.append(copy)
            dual_sq += jnp.sum((after - now) ** 2, axis=0, keepdims=True)
        res_send[turn : turn + 1] = weight[...] * primal_sq + dual_sq / weight[...]

    def res_copy(k):
        return pltpu.make_async_remote_copy(
            src_ref=res_send,
            dst_ref=res_recv.at[k],
            send_sem=res_send_sem.at[k],
            recv_sem=res_recv_sem.at[k],
            device_id={"col": lax.rem(me + k, n)},
            device_id_type=MESH,
        )

    def spread(k, carry):
        res_copy(lax.rem(k + n // 2 - 1, n - 1) + 1).start()
        return carry

    lax.fori_loop(1, n, spread, 0)
    res_recv[0] = res_send[...]
    for copy in sent:
        copy.wait_send()

    def collect(k, carry):
        res_copy(k).wait()
        return carry

    lax.fori_loop(1, n, collect, 0)
    total = jnp.sum(res_recv[...], axis=0)
    cells = jnp.float32((ncols + nrows) * n)
    residual_out[...] = jnp.sqrt(total / cells)


def per_device(
    blocks,
    block_rows,
    block_cols,
    primal,
    dual,
    anchor_primal,
    anchor_dual,
    cost,
    rhs,
    bound_kind,
    lower,
    upper,
    step_size,
    primal_weight,
):
    n = lax.axis_size("col")
    nz, size, _ = blocks.shape
    ncols, inst = primal.shape
    nrows = dual.shape[0]
    part = nrows // CHUNKS
    f32, bf16, i32 = jnp.float32, jnp.bfloat16, jnp.int32
    any_space = pl.BlockSpec(memory_space=pl.ANY)
    vmem = pltpu.VMEM
    dma = pltpu.SemaphoreType.DMA
    return pl.pallas_call(
        functools.partial(kernel, n),
        out_shape=(
            vmem((ncols, inst), f32),
            vmem((nrows, inst), f32),
            vmem((ITERS, inst), f32),
        ),
        in_specs=[any_space] * 14,
        out_specs=(pl.BlockSpec(memory_space=vmem),) * 3,
        scratch_shapes=[
            vmem((nz + 1, size, size), bf16),
            vmem((nz + 1, size, size), bf16),
            vmem((1, nz), i32),
            vmem((1, nz), i32),
            vmem((1, 128), i32),
            pltpu.SMEM((1, 128), i32),
            vmem((3 * nrows, ncols), bf16),
            vmem((ncols, 3 * nrows), bf16),
            vmem((ncols, inst), f32),
            vmem((ncols, inst), f32),
            vmem((ncols, inst), f32),
            vmem((ncols, inst), i32),
            vmem((ncols, inst), f32),
            vmem((ncols, inst), f32),
            vmem((ncols // size, size), f32),
            vmem((ncols // size, size), f32),
            vmem((ncols, inst), f32),
            vmem((ncols, inst), bf16),
            vmem((ncols, inst), f32),
            vmem((nrows, inst), f32),
            vmem((nrows, inst), f32),
            vmem((ITERS, CHUNKS, part, inst), bf16),
            vmem((ITERS, 2, CHUNKS, part, inst), bf16),
            vmem((nrows, inst), f32),
            vmem((ITERS, CHUNKS, part, inst), bf16),
            vmem((ITERS, CHUNKS, part, inst), bf16),
            vmem((ITERS, CHUNKS, part, inst), f32),
            vmem((ITERS, CHUNKS, part, inst), f32),
            vmem((1, inst), f32),
            vmem((1, inst), f32),
            vmem((ITERS, inst), f32),
            vmem((n, ITERS, inst), f32),
            dma((14,)),
            dma((ITERS, 2, CHUNKS)),
            dma((ITERS, 2, CHUNKS)),
            dma((ITERS, 2, CHUNKS)),
            dma((ITERS, 2, CHUNKS)),
            dma((n,)),
            dma((n,)),
            dma,
        ],
        compiler_params=pltpu.CompilerParams(
            collective_id=0, has_side_effects=True, vmem_limit_bytes=56 * 1024 * 1024
        ),
        cost_estimate=pl.CostEstimate(
            flops=4 * ITERS * nz * size * size * inst, bytes_accessed=6 * 2**20, transcendentals=0
        ),
    )(
        blocks,
        block_rows.reshape(1, nz),
        block_cols.reshape(1, nz),
        primal,
        dual,
        anchor_primal,
        anchor_dual,
        cost,
        rhs,
        bound_kind,
        lower.reshape(ncols // size, size),
        upper.reshape(ncols // size, size),
        step_size.reshape(1, inst),
        primal_weight.reshape(1, inst),
    )


def solution(mesh):
    return jax.shard_map(
        per_device,
        mesh=mesh,
        in_specs=(
            P("col", None, None),
            P("col"),
            P("col"),
            P("col", "groups"),
            P("col", "groups"),
            P("col", "groups"),
            P("col", "groups"),
            P("col", "groups"),
            P("col", "groups"),
            P("col", "groups"),
            P("col"),
            P("col"),
            P("groups"),
            P("groups"),
        ),
        out_specs=(P("col", "groups"), P("col", "groups"), P(None, "groups")),
        check_vma=False,
    )
```
